32 devices in a mesh: ka: 8 (over z, y), ba: 4 (over x, core).
Axes of the slice: x: 2, y: 2, z: 4, core: 2. Of those that a mesh axis runs over, the one named last changes fastest.
Arguments:
- green_irr: bfloat16 [8, 2, 768, 768], P('ka', None, 'ba'), may hold values from -48 to 48
- screened: bfloat16 [128, 768, 768], P('ka', 'ba'), may hold values from -0.75 to 0.75
- kmap: int32 [128, 1], replicated, may hold values from 0 to 7
- rotation: int32 [128, 768], replicated, may hold values from -768 to 767, as said below
Outputs:
- sigma_irr: float32 [8, 2, 768, 768], P('ka', None, 'ba')
The draws below stay inside these ranges and needn't reach their ends.
Inputs may be any that keep to these rules, and one draw needn't show every extreme that they name: `kmap`: each of the 8 irreducible points is named by one or more k-points. `rotation`: for every k, the sources of the 768 functions are a permutation of them that maps the 6 functions of each atom among themselves (atom n holds functions n * 6 to n * 6 + 5); v >= 0 means source v with sign 1, v < 0 means source -1 - v with sign -1.
All inputs are finite; a program needn't handle non-finite values.
Results may differ from the reference program's by a relative error of at most 0.0065.
Values may be sent and summed in bfloat16 or wider, within the bound.
A program may use at most 64 MiB of HBM per device.

```python
import math
import jax
import jax.numpy as jnp
from jax import lax

NATOM = 128
NORB = 6
KX = 8
KY = 4
KZ = 4
NB = 768
NK = 128
NIR = 8


def draw_rotation(key, part):
    key = jax.random.fold_in(key, 7)
    first, second = jax.random.split(key)
    scores = jax.random.randint(first, (NK, NATOM, NORB), 0, 1 << 20)
    scores = scores * NORB + jnp.arange(NORB, dtype=jnp.int32)[None, None, :]
    order = jnp.argsort(scores, axis=-1).astype(jnp.int32)
    base = (jnp.arange(NATOM, dtype=jnp.int32) * NORB)[None, :, None]
    source = (order + base).reshape(NK, NATOM * NORB)
    flips = jax.random.randint(second, (NK, NATOM * NORB), 0, 2)
    return jnp.where(flips == 1, -1 - source, source).astype(jnp.int32)


def level_of(own_key, shape, cuts, least, top_value):
    loudness = 1.0
    for position, blocks in cuts:
        heights = jax.random.uniform(jax.random.fold_in(jax.random.fold_in(own_key, 6), position), (blocks,), jnp.float32, least / len(cuts), top_value / len(cuts))
        loudness = loudness * jnp.repeat(jnp.exp(heights), shape[position] // blocks).reshape((-1,) + (1,) * (len(shape) - 1 - position))
    return loudness


def distinct(rng, rows, count, top, lift):
    order = jax.random.permutation(jax.random.fold_in(rng, 1), count)
    boost = order
    for power in range(3):
        boost = boost * boost // count
    boost = boost * lift // count
    lots = jax.random.randint(jax.random.fold_in(rng, 2), (rows, count), 0, 4096) + boost
    fixed_rows = jax.random.permutation(jax.random.fold_in(rng, 3), rows)[jnp.arange(count) % rows]
    lots = jnp.where(jnp.arange(rows)[:, None] == fixed_rows[None, :], 1 << 14, lots)
    merit = lots * count + jnp.arange(count)
    return lax.top_k(merit.astype(jnp.int32), top)[1].astype(jnp.int32)


def normal_values(key, extent, deviation, reach, shards=(), kind=jnp.bfloat16):
    array = deviation * jax.random.normal(key, extent, jnp.float32)
    if shards:
        array = array * level_of(key, extent, shards, -0.22, 0.18)
    return jnp.clip(array, -reach, reach).astype(kind)


def setup_inputs(seed: int = 0) -> dict:
    seeds = jax.random.split(jax.random.key(seed), 5)
    return {
        "green_irr": normal_values(seeds[0], (NIR, 2, NB, NB), 8.0, 48.0, ((0, 8), (2, 4))),
        "screened": normal_values(seeds[1], (NK, NB, NB), 0.125, 0.75, ((0, 8), (1, 4))),
        "kmap": distinct(seeds[2], NK, NIR, 1, 2048),
        "rotation": draw_rotation(jax.random.fold_in(seeds[4], 71), 0),
    }


def decode(rotation):
    source = jnp.where(rotation >= 0, rotation, -1 - rotation).astype(jnp.int32)
    signs = jnp.where(rotation >= 0, 1.0, -1.0).astype(jnp.bfloat16)
    return source, signs


def phase_tables(count):
    index = jnp.arange(count, dtype=jnp.int32)
    first = index // (KY * KZ)
    second = (index // KZ) % KY
    third = index % KZ
    turns = first[:, None] * first[None, :] + second[:, None] * second[None, :] * (KX // KY)
    turns = (turns + third[:, None] * third[None, :] * (KX // KZ)) % KX
    angle = turns.astype(jnp.float32) * (2.0 * math.pi / KX)
    return jnp.cos(angle).astype(jnp.bfloat16), jnp.sin(angle).astype(jnp.bfloat16)


def rotate_block(block, row_index, col_index, row_signs, col_signs):
    picked = jnp.take(jnp.take(block, row_index, axis=1), col_index, axis=2)
    return picked * (row_signs[:, None] * col_signs[None, :])[None]


def reference(green_irr, screened, kmap, rotation):
    targets = kmap[:, 0].astype(jnp.int32)
    source, signs = decode(rotation)
    every_k = jnp.arange(NK, dtype=jnp.int32)
    every_b = jnp.arange(NB, dtype=jnp.int32)
    inverse = jnp.zeros_like(source).at[every_k[:, None], source].set(jnp.broadcast_to(every_b[None, :], (NK, NB)))
    inv_signs = jnp.take_along_axis(signs, inverse, axis=1)
    cos_t, sin_t = phase_tables(NK)
    counts = jnp.sum((targets[:, None] == jnp.arange(NIR, dtype=jnp.int32)[None, :]).astype(jnp.float32), axis=0)
    block = NB // 8

    def unfold_one(target, row_index, col_index, row_signs, col_signs):
        whole = lax.dynamic_index_in_dim(green_irr, target, 0, keepdims=False)
        return rotate_block(whole, row_index, col_index, row_signs, col_signs)

    def one_block(number):
        offset = number * block
        rows_here = offset + jnp.arange(block, dtype=jnp.int32)
        green_k = jax.vmap(unfold_one)(targets, source[:, rows_here], source, signs[:, rows_here], signs)
        flat = green_k.reshape(NK, 2, block * NB)
        green_r = ((jnp.dot(cos_t, flat[:, 0], preferred_element_type=jnp.float32)
                    - jnp.dot(sin_t, flat[:, 1], preferred_element_type=jnp.float32)) * (1.0 / NK)).astype(jnp.bfloat16)
        w_here = screened[:, rows_here].reshape(NK, block * NB)
        sigma_r = (-(green_r.astype(jnp.float32) * w_here.astype(jnp.float32))).astype(jnp.bfloat16)
        real_k = jnp.dot(cos_t, sigma_r, preferred_element_type=jnp.float32).astype(jnp.bfloat16)
        imag_k = (-jnp.dot(sin_t, sigma_r, preferred_element_type=jnp.float32)).astype(jnp.bfloat16)
        sigma_k = jnp.stack([real_k, imag_k], axis=1).reshape(NK, 2, block, NB)
        inv_here = inverse[:, rows_here] - offset
        turned = jax.vmap(rotate_block)(sigma_k, inv_here, inverse, inv_signs[:, rows_here], inv_signs)
        summed = jax.ops.segment_sum(turned.astype(jnp.float32), targets, NIR)
        return summed / counts[:, None, None, None]

    pieces = lax.map(one_block, jnp.arange(8, dtype=jnp.int32))
    return jnp.moveaxis(pieces, 0, 2).reshape(NIR, 2, NB, NB)
```

```python
import math

import jax
import jax.numpy as jnp
from jax import lax
from jax.experimental import pallas as pl
from jax.experimental.pallas import tpu as pltpu
from jax.sharding import PartitionSpec as P

KX = 8
KY = 4
KZ = 4


def decode(rotation):
    source = jnp.where(rotation >= 0, rotation, -1 - rotation)
    signs = jnp.where(rotation >= 0, 1.0, -1.0).astype(jnp.bfloat16)
    return (source, signs)


def phase_tables(count):
    index = jnp.arange(count, dtype=jnp.int32)
    first = index // (KY * KZ)
    second = index // KZ % KY
    third = index % KZ
    turns = first[:, None] * first[None, :] + second[:, None] * second[None, :] * (KX // KY)
    turns = (turns + third[:, None] * third[None, :] * (KX // KZ)) % KX
    angle = turns.astype(jnp.float32) * (2.0 * math.pi / KX)
    return (jnp.cos(angle).astype(jnp.bfloat16), jnp.sin(angle).astype(jnp.bfloat16))


def turn_tables(local_source, local_signs, width):
    places = jnp.arange(width, dtype=jnp.int32)
    same = (local_source[:, :, None] == places[None, None, :]).astype(jnp.bfloat16)
    return same * local_signs[:, :, None]


def turn_forward(block, row_turn, col_turn):
    half = jnp.einsum("kab,kcbd->kcad", row_turn, block, preferred_element_type=jnp.float32).astype(
        jnp.bfloat16
    )
    return jnp.einsum("kcad,ked->kcae", half, col_turn, preferred_element_type=jnp.float32).astype(
        jnp.bfloat16
    )


def turn_back(block, row_turn, col_turn):
    half = jnp.einsum("kab,kcad->kcbd", row_turn, block, preferred_element_type=jnp.float32).astype(
        jnp.bfloat16
    )
    return jnp.einsum("kcbd,kde->kcbe", half, col_turn, preferred_element_type=jnp.float32).astype(
        jnp.bfloat16
    )


def per_device_columns(green_irr, screened, kmap, rotation):
    width_ka = lax.axis_size("ka")
    place_ka = lax.axis_index("ka")
    place_ba = lax.axis_index("ba")
    zone = rotation.shape[0]
    basis = rotation.shape[1]
    rows = green_irr.shape[2]
    cols = basis // width_ka
    wedges = green_irr.shape[0] * width_ka
    row_start = place_ba * rows
    col_start = place_ka * cols
    targets = kmap[:, 0]
    source, signs = decode(rotation)
    cos_t, sin_t = phase_tables(zone)
    counts = jnp.sum(
        (targets[:, None] == jnp.arange(wedges, dtype=jnp.int32)[None, :]).astype(jnp.float32),
        axis=0,
    )
    src_rows = lax.dynamic_slice_in_dim(source, row_start, rows, 1) - row_start
    sgn_rows = lax.dynamic_slice_in_dim(signs, row_start, rows, 1)
    moved = lax.all_to_all(green_irr, "ka", split_axis=3, concat_axis=0, tiled=True)
    src_cols = lax.dynamic_slice_in_dim(source, col_start, cols, 1) - col_start
    sgn_cols = lax.dynamic_slice_in_dim(signs, col_start, cols, 1)
    row_turn = turn_tables(src_rows, sgn_rows, rows)
    col_turn = turn_tables(src_cols, sgn_cols, cols)
    pick = (targets[:, None] == jnp.arange(wedges, dtype=jnp.int32)[None, :]).astype(jnp.bfloat16)
    selected = jnp.einsum("kn,ncab->kcab", pick, moved, preferred_element_type=jnp.float32).astype(
        jnp.bfloat16
    )
    green_k = turn_forward(selected, row_turn, col_turn)
    flat = green_k.reshape(zone, 2, rows * cols)
    green_r = (
        (
            jnp.dot(cos_t, flat[:, 0], preferred_element_type=jnp.float32)
            - jnp.dot(sin_t, flat[:, 1], preferred_element_type=jnp.float32)
        )
        * (1.0 / zone)
    ).astype(jnp.bfloat16)
    at_lattice = lax.all_to_all(
        green_r.reshape(zone, rows, cols), "ka", split_axis=0, concat_axis=2, tiled=True
    )
    product = (-(at_lattice.astype(jnp.float32) * screened.astype(jnp.float32))).astype(
        jnp.bfloat16
    )
    sigma_r = lax.all_to_all(product, "ka", split_axis=2, concat_axis=0, tiled=True).reshape(
        zone, rows * cols
    )
    real_k = jnp.dot(cos_t, sigma_r, preferred_element_type=jnp.float32).astype(jnp.bfloat16)
    imag_k = (-jnp.dot(sin_t, sigma_r, preferred_element_type=jnp.float32)).astype(jnp.bfloat16)
    sigma_k = jnp.stack([real_k, imag_k], axis=1).reshape(zone, 2, rows, cols)
    turned = turn_back(sigma_k, row_turn, col_turn)
    hit = (targets[None, :] == jnp.arange(wedges, dtype=jnp.int32)[:, None]).astype(jnp.bfloat16)
    folded = jnp.einsum("ik,kcab->icab", hit, turned, preferred_element_type=jnp.float32)
    folded = folded / counts[:, None, None, None]
    return lax.all_to_all(
        folded.astype(jnp.bfloat16), "ka", split_axis=0, concat_axis=3, tiled=True
    ).astype(folded.dtype)


ORB = 6


def column_order(basis):
    atoms = basis // ORB
    place = jnp.arange(basis, dtype=jnp.int32)
    moved = (place % ORB) * atoms + place // ORB
    return (moved[:, None] == place[None, :]).astype(jnp.bfloat16)


def prepare_kernel(swap_ref, order_ref, w_ref, out_ref):
    count, rows, basis = w_ref.shape
    block = w_ref[...].reshape(count * rows, basis)
    turned = jnp.dot(swap_ref[...], block, preferred_element_type=jnp.float32).astype(jnp.bfloat16)
    out = jnp.dot(turned, order_ref[...], preferred_element_type=jnp.float32).astype(jnp.bfloat16)
    out_ref[...] = out.reshape(rows, count, basis)


def prepare(screened, order, step=16):
    count, rows, basis = screened.shape
    place = jnp.arange(count * step, dtype=jnp.int32)
    origin = (place % count) * step + place // count
    swap = (origin[:, None] == place[None, :]).astype(jnp.bfloat16)
    return pl.pallas_call(
        prepare_kernel,
        grid=(rows // step,),
        in_specs=[
            pl.BlockSpec((count * step, count * step), lambda i: (0, 0)),
            pl.BlockSpec((basis, basis), lambda i: (0, 0)),
            pl.BlockSpec((count, step, basis), lambda i: (0, i, 0)),
        ],
        out_specs=pl.BlockSpec((step, count, basis), lambda i: (i, 0, 0)),
        out_shape=jax.ShapeDtypeStruct((rows, count, basis), jnp.bfloat16),
        compiler_params=pltpu.CompilerParams(vmem_limit_bytes=24 << 20),
        cost_estimate=pl.CostEstimate(
            flops=4800000000, bytes_accessed=4 * count * rows * basis, transcendentals=0
        ),
    )(swap, order, screened)


def turn_columns(coef_ref, src, dst, zone, atoms, back):
    def chunk(step, carry):
        at = pl.ds(pl.multiple_of(step * 16, 16), 16)
        coef = [[coef_ref[o, p, at, :] for p in range(ORB)] for o in range(ORB)]
        for oa in range(ORB):
            for c in range(2):
                given = [src(oa, c, p, step) for p in range(ORB)]
                for o in range(ORB):
                    total = None
                    for p in range(ORB):
                        term = (coef[p][o] if back else coef[o][p]) * given[p]
                        total = term if total is None else total + term
                    dst(oa, c, o, step, total)
        return carry

    lax.fori_loop(0, zone // 16, chunk, 0)


def unfold_kernel(select_ref, green_ref, coef_ref, phase_ref, out_ref, half, full):
    zone = phase_ref.shape[0]
    basis = out_ref.shape[2]
    atoms = basis // ORB
    half[...] = jnp.dot(select_ref[0], green_ref[0], preferred_element_type=jnp.float32).astype(
        jnp.bfloat16
    )

    def read(oa, c, p, step):
        at = pl.ds(pl.multiple_of(oa * zone + step * 16, 16), 16)
        return half[at, c * basis + p * atoms : c * basis + (p + 1) * atoms]

    def write(oa, c, o, step, value):
        at = pl.ds(pl.multiple_of(c * zone + step * 16, 16), 16)
        full[oa, at, o * atoms : (o + 1) * atoms] = value

    turn_columns(coef_ref, read, write, zone, atoms, False)
    for oa in range(ORB):
        sums = jnp.dot(phase_ref[...], full[oa], preferred_element_type=jnp.float32)
        out_ref[oa] = (sums * (1.0 / zone)).astype(jnp.bfloat16)


def fold_kernel(select_ref, counts_ref, green_ref, w_ref, coef_ref, phase_ref, out_ref, full, half):
    zone = phase_ref.shape[1]
    basis = green_ref.shape[2]
    atoms = basis // ORB
    for oa in range(ORB):
        w = w_ref[:, oa].reshape(zone, basis)
        sigma = (-(green_ref[oa].astype(jnp.float32) * w.astype(jnp.float32))).astype(jnp.bfloat16)
        full[oa] = jnp.dot(phase_ref[...], sigma, preferred_element_type=jnp.float32).astype(
            jnp.bfloat16
        )

    def read(oa, c, p, step):
        at = pl.ds(pl.multiple_of(c * zone + step * 16, 16), 16)
        return full[oa, at, p * atoms : (p + 1) * atoms]

    def write(oa, c, o, step, value):
        at = pl.ds(pl.multiple_of(oa * zone + step * 16, 16), 16)
        half[at, c * basis + o * atoms : c * basis + (o + 1) * atoms] = value

    turn_columns(coef_ref, read, write, zone, atoms, True)
    sums = jnp.dot(select_ref[0], half[...], preferred_element_type=jnp.float32)
    out_ref[0] = (sums / counts_ref[...]).astype(jnp.bfloat16)


def per_device_rows(green_irr, screened, kmap, rotation):
    width = lax.axis_size("ka")
    zone, basis = rotation.shape
    atoms = basis // ORB
    own, _, rows, _ = green_irr.shape
    wedges = own * width
    part = rows // width
    sites = part // ORB
    near = screened.shape[0]
    targets = kmap[:, 0]
    order = column_order(basis)

    sent = prepare(screened, order).reshape(width, part, near, basis)
    w = lax.all_to_all(sent, "ka", split_axis=0, concat_axis=0, tiled=True)

    green = jnp.dot(
        green_irr.reshape(own * 2 * rows, basis), order, preferred_element_type=jnp.float32
    ).astype(jnp.bfloat16)
    green = green.reshape(own, 2, width, part, basis).transpose(2, 0, 1, 3, 4)
    green = lax.all_to_all(green, "ka", split_axis=0, concat_axis=0, tiled=True)
    green = green.reshape(wedges, 2, sites, ORB, basis).transpose(2, 0, 3, 1, 4)
    green = green.reshape(sites, wedges * ORB, 2 * basis)

    cos_t, sin_t = phase_tables(zone)
    source, signs = decode(rotation)
    orbital = jnp.arange(ORB, dtype=jnp.int32)
    place = source - (jnp.arange(basis, dtype=jnp.int32) // ORB * ORB)[None, :]
    place = place.reshape(zone, atoms, ORB).transpose(2, 0, 1)
    sign = signs.reshape(zone, atoms, ORB).transpose(2, 0, 1)
    coef = (place[:, None] == orbital[None, :, None, None]).astype(jnp.bfloat16) * sign[:, None]

    first = lax.axis_index("ba") * rows // ORB + lax.axis_index("ka") * sites
    row_place = lax.dynamic_slice_in_dim(place, first, sites, 2).transpose(2, 0, 1)
    row_sign = lax.dynamic_slice_in_dim(sign, first, sites, 2).transpose(2, 0, 1)
    code = targets[None, None, :] * ORB + row_place
    hit = jnp.arange(wedges * ORB, dtype=jnp.int32)
    code = code.reshape(sites, ORB * zone)
    row_sign = row_sign.reshape(sites, ORB * zone)
    select = (code[:, :, None] == hit[None, None, :]).astype(jnp.bfloat16) * row_sign[:, :, None]
    back = (code[:, None, :] == hit[None, :, None]).astype(jnp.bfloat16) * row_sign[:, None, :]
    counts = jnp.sum(
        (targets[None, :] == (hit // ORB)[:, None]).astype(jnp.float32), axis=1, keepdims=True
    )

    whole = lambda shape: pl.BlockSpec(shape, lambda i: (0,) * len(shape))
    params = pltpu.CompilerParams(vmem_limit_bytes=40 << 20)
    cost = pl.CostEstimate(flops=12000000000, bytes_accessed=12 << 20, transcendentals=0)
    green_r = pl.pallas_call(
        unfold_kernel,
        grid=(sites,),
        in_specs=[
            pl.BlockSpec((1, ORB * zone, wedges * ORB), lambda i: (i, 0, 0)),
            pl.BlockSpec((1, wedges * ORB, 2 * basis), lambda i: (i, 0, 0)),
            whole(coef.shape),
            whole((zone, 2 * zone)),
        ],
        out_specs=pl.BlockSpec((ORB, zone, basis), lambda i: (i, 0, 0)),
        out_shape=jax.ShapeDtypeStruct((part, zone, basis), jnp.bfloat16),
        scratch_shapes=[
            pltpu.VMEM((ORB * zone, 2 * basis), jnp.bfloat16),
            pltpu.VMEM((ORB, 2 * zone, basis), jnp.bfloat16),
        ],
        compiler_params=params,
        cost_estimate=cost,
    )(select, green, coef, jnp.concatenate([cos_t, -sin_t], axis=1))
    folded = pl.pallas_call(
        fold_kernel,
        grid=(sites,),
        in_specs=[
            pl.BlockSpec((1, wedges * ORB, ORB * zone), lambda i: (i, 0, 0)),
            whole((wedges * ORB, 1)),
            pl.BlockSpec((ORB, zone, basis), lambda i: (i, 0, 0)),
            pl.BlockSpec((width, ORB, near, basis), lambda i: (0, i, 0, 0)),
            whole(coef.shape),
            whole((2 * zone, zone)),
        ],
        out_specs=pl.BlockSpec((1, wedges * ORB, 2 * basis), lambda i: (i, 0, 0)),
        out_shape=jax.ShapeDtypeStruct((sites, wedges * ORB, 2 * basis), jnp.bfloat16),
        scratch_shapes=[
            pltpu.VMEM((ORB, 2 * zone, basis), jnp.bfloat16),
            pltpu.VMEM((ORB * zone, 2 * basis), jnp.bfloat16),
        ],
        compiler_params=params,
        cost_estimate=cost,
    )(back, counts, green_r, w, coef, jnp.concatenate([cos_t, -sin_t], axis=0))

    folded = folded.reshape(sites, wedges, ORB, 2, basis).transpose(1, 3, 0, 2, 4)
    folded = folded.reshape(width, own, 2, part, basis)
    folded = lax.all_to_all(folded, "ka", split_axis=0, concat_axis=0, tiled=True)
    folded = folded.transpose(1, 2, 0, 3, 4).reshape(own * 2 * rows, basis)
    out = lax.dot_general(
        folded, order, (((1,), (1,)), ((), ())), preferred_element_type=jnp.float32
    )
    return out.reshape(own, 2, rows, basis)


def per_device(green_irr, screened, kmap, rotation):
    rows = green_irr.shape[2]
    width = lax.axis_size("ka")
    if rows % (width * ORB) == 0 and screened.shape[0] % 16 == 0:
        return per_device_rows(green_irr, screened, kmap, rotation)
    return per_device_columns(green_irr, screened, kmap, rotation)


def solution(mesh):
    placed = (P("ka", None, "ba", None), P("ka", "ba", None), P(), P())
    return jax.shard_map(
        per_device, mesh=mesh, in_specs=placed, out_specs=P("ka", None, "ba", None), check_vma=False
    )
```

```python
import math

import jax
import jax.numpy as jnp
from jax import lax
from jax.experimental import pallas as pl
from jax.experimental.pallas import tpu as pltpu
from jax.sharding import Mesh
from jax.sharding import PartitionSpec as P

KX = 8
KY = 4
KZ = 4


def decode(rotation):
    source = jnp.where(rotation >= 0, rotation, -1 - rotation)
    signs = jnp.where(rotation >= 0, 1.0, -1.0).astype(jnp.bfloat16)
    return (source, signs)


def phase_tables(count):
    index = jnp.arange(count, dtype=jnp.int32)
    first = index // (KY * KZ)
    second = index // KZ % KY
    third = index % KZ
    turns = first[:, None] * first[None, :] + second[:, None] * second[None, :] * (KX // KY)
    turns = (turns + third[:, None] * third[None, :] * (KX // KZ)) % KX
    angle = turns.astype(jnp.float32) * (2.0 * math.pi / KX)
    return (jnp.cos(angle).astype(jnp.bfloat16), jnp.sin(angle).astype(jnp.bfloat16))


def turn_tables(local_source, local_signs, width):
    places = jnp.arange(width, dtype=jnp.int32)
    same = (local_source[:, :, None] == places[None, None, :]).astype(jnp.bfloat16)
    return same * local_signs[:, :, None]


def turn_forward(block, row_turn, col_turn):
    half = jnp.einsum("kab,kcbd->kcad", row_turn, block, preferred_element_type=jnp.float32).astype(
        jnp.bfloat16
    )
    return jnp.einsum("kcad,ked->kcae", half, col_turn, preferred_element_type=jnp.float32).astype(
        jnp.bfloat16
    )


def turn_back(block, row_turn, col_turn):
    half = jnp.einsum("kab,kcad->kcbd", row_turn, block, preferred_element_type=jnp.float32).astype(
        jnp.bfloat16
    )
    return jnp.einsum("kcbd,kde->kcbe", half, col_turn, preferred_element_type=jnp.float32).astype(
        jnp.bfloat16
    )


def per_device_columns(green_irr, screened, kmap, rotation):
    width_ka = lax.axis_size("ka")
    place_ka = lax.axis_index("ka")
    place_ba = lax.axis_index("ba")
    zone = rotation.shape[0]
    basis = rotation.shape[1]
    rows = green_irr.shape[2]
    cols = basis // width_ka
    wedges = green_irr.shape[0] * width_ka
    row_start = place_ba * rows
    col_start = place_ka * cols
    targets = kmap[:, 0]
    source, signs = decode(rotation)
    cos_t, sin_t = phase_tables(zone)
    counts = jnp.sum(
        (targets[:, None] == jnp.arange(wedges, dtype=jnp.int32)[None, :]).astype(jnp.float32),
        axis=0,
    )
    src_rows = lax.dynamic_slice_in_dim(source, row_start, rows, 1) - row_start
    sgn_rows = lax.dynamic_slice_in_dim(signs, row_start, rows, 1)
    moved = lax.all_to_all(green_irr, "ka", split_axis=3, concat_axis=0, tiled=True)
    src_cols = lax.dynamic_slice_in_dim(source, col_start, cols, 1) - col_start
    sgn_cols = lax.dynamic_slice_in_dim(signs, col_start, cols, 1)
    row_turn = turn_tables(src_rows, sgn_rows, rows)
    col_turn = turn_tables(src_cols, sgn_cols, cols)
    pick = (targets[:, None] == jnp.arange(wedges, dtype=jnp.int32)[None, :]).astype(jnp.bfloat16)
    selected = jnp.einsum("kn,ncab->kcab", pick, moved, preferred_element_type=jnp.float32).astype(
        jnp.bfloat16
    )
    green_k = turn_forward(selected, row_turn, col_turn)
    flat = green_k.reshape(zone, 2, rows * cols)
    green_r = (
        (
            jnp.dot(cos_t, flat[:, 0], preferred_element_type=jnp.float32)
            - jnp.dot(sin_t, flat[:, 1], preferred_element_type=jnp.float32)
        )
        * (1.0 / zone)
    ).astype(jnp.bfloat16)
    at_lattice = lax.all_to_all(
        green_r.reshape(zone, rows, cols), "ka", split_axis=0, concat_axis=2, tiled=True
    )
    product = (-(at_lattice.astype(jnp.float32) * screened.astype(jnp.float32))).astype(
        jnp.bfloat16
    )
    sigma_r = lax.all_to_all(product, "ka", split_axis=2, concat_axis=0, tiled=True).reshape(
        zone, rows * cols
    )
    real_k = jnp.dot(cos_t, sigma_r, preferred_element_type=jnp.float32).astype(jnp.bfloat16)
    imag_k = (-jnp.dot(sin_t, sigma_r, preferred_element_type=jnp.float32)).astype(jnp.bfloat16)
    sigma_k = jnp.stack([real_k, imag_k], axis=1).reshape(zone, 2, rows, cols)
    turned = turn_back(sigma_k, row_turn, col_turn)
    hit = (targets[None, :] == jnp.arange(wedges, dtype=jnp.int32)[:, None]).astype(jnp.bfloat16)
    folded = jnp.einsum("ik,kcab->icab", hit, turned, preferred_element_type=jnp.float32)
    folded = folded / counts[:, None, None, None]
    return lax.all_to_all(
        folded.astype(jnp.bfloat16), "ka", split_axis=0, concat_axis=3, tiled=True
    ).astype(folded.dtype)


ORB = 6


def column_order(basis):
    atoms = basis // ORB
    place = jnp.arange(basis, dtype=jnp.int32)
    moved = (place % ORB) * atoms + place // ORB
    return (moved[:, None] == place[None, :]).astype(jnp.bfloat16)


def prepare_kernel(swap_ref, order_ref, w_ref, *out_refs):
    count, rows, basis = w_ref.shape
    step = swap_ref.shape[0] // count
    each = rows // len(out_refs)
    for start in range(0, rows, step):
        block = w_ref[:, start : start + step, :].reshape(count * step, basis)
        turned = jnp.dot(swap_ref[...], block, preferred_element_type=jnp.float32)
        out = jnp.dot(
            turned.astype(jnp.bfloat16), order_ref[...], preferred_element_type=jnp.float32
        ).astype(jnp.bfloat16)
        out = out.reshape(step, count, basis)
        for row in range(start, start + step):
            out_refs[row // each][0, row % each] = out[row - start]


def prepare(screened, order, width, pieces, step=16):
    count, rows, basis = screened.shape
    part = rows // width
    each = part // pieces
    place = jnp.arange(count * step, dtype=jnp.int32)
    origin = (place % count) * step + place // count
    swap = (origin[:, None] == place[None, :]).astype(jnp.bfloat16)
    return pl.pallas_call(
        prepare_kernel,
        grid=(width,),
        in_specs=[
            pl.BlockSpec((count * step, count * step), lambda i: (0, 0)),
            pl.BlockSpec((basis, basis), lambda i: (0, 0)),
            pl.BlockSpec((count, part, basis), lambda i: (0, i, 0)),
        ],
        out_specs=[pl.BlockSpec((1, each, count, basis), lambda i: (i, 0, 0, 0))] * pieces,
        out_shape=[jax.ShapeDtypeStruct((width, each, count, basis), jnp.bfloat16)] * pieces,
        compiler_params=pltpu.CompilerParams(vmem_limit_bytes=24 << 20),
        cost_estimate=pl.CostEstimate(
            flops=4800000000, bytes_accessed=4 * count * rows * basis, transcendentals=0
        ),
    )(swap, order, screened)


def turn_columns(coef_ref, src, dst, zone, atoms, back):
    def chunk(step, carry):
        at = pl.ds(pl.multiple_of(step * 16, 16), 16)
        coef = [[coef_ref[o, p, at, :] for p in range(ORB)] for o in range(ORB)]
        for oa in range(ORB):
            for c in range(2):
                given = [src(oa, c, p, step) for p in range(ORB)]
                for o in range(ORB):
                    total = None
                    for p in range(ORB):
                        term = (coef[p][o] if back else coef[o][p]) * given[p]
                        total = term if total is None else total + term
                    dst(oa, c, o, step, total)
        return carry

    lax.fori_loop(0, zone // 16, chunk, 0)


def unfold_kernel(select_ref, green_ref, coef_ref, phase_ref, out_ref, half, full):
    zone = phase_ref.shape[1] // 2
    basis = out_ref.shape[2]
    atoms = basis // ORB
    half[...] = jnp.dot(select_ref[0], green_ref[0], preferred_element_type=jnp.float32).astype(
        jnp.bfloat16
    )

    def read(oa, c, p, step):
        at = pl.ds(pl.multiple_of(oa * zone + step * 16, 16), 16)
        return half[at, c * basis + p * atoms : c * basis + (p + 1) * atoms]

    def write(oa, c, o, step, value):
        at = pl.ds(pl.multiple_of(c * zone + step * 16, 16), 16)
        full[oa, at, o * atoms : (o + 1) * atoms] = value

    turn_columns(coef_ref, read, write, zone, atoms, False)
    for oa in range(ORB):
        sums = jnp.dot(phase_ref[...], full[oa], preferred_element_type=jnp.float32)
        out_ref[oa] = (sums * (1.0 / zone)).astype(jnp.bfloat16)


def fold_kernel(select_ref, counts_ref, green_ref, w_ref, coef_ref, phase_ref, out_ref, full, half):
    near = phase_ref.shape[1]
    zone = phase_ref.shape[0] // 2
    basis = green_ref.shape[2]
    atoms = basis // ORB
    for oa in range(ORB):
        w = w_ref[:, oa].reshape(near, basis)
        sigma = (-(green_ref[oa].astype(jnp.float32) * w.astype(jnp.float32))).astype(jnp.bfloat16)
        full[oa] = jnp.dot(phase_ref[...], sigma, preferred_element_type=jnp.float32).astype(
            jnp.bfloat16
        )

    def read(oa, c, p, step):
        at = pl.ds(pl.multiple_of(c * zone + step * 16, 16), 16)
        return full[oa, at, p * atoms : (p + 1) * atoms]

    def write(oa, c, o, step, value):
        at = pl.ds(pl.multiple_of(oa * zone + step * 16, 16), 16)
        half[at, c * basis + o * atoms : c * basis + (o + 1) * atoms] = value

    turn_columns(coef_ref, read, write, zone, atoms, True)
    sums = jnp.dot(select_ref[0], half[...], preferred_element_type=jnp.float32)
    out_ref[0] = (sums / counts_ref[...]).astype(jnp.bfloat16)


PIECES = 2
HALVES = 2


def per_device_rows(green_irr, screened, kmap, rotation):
    halves = lax.axis_size("kh")
    width = lax.axis_size("kl")
    both = ("kh", "kl")
    zone, basis = rotation.shape
    atoms = basis // ORB
    own, _, rows, _ = green_irr.shape
    wedges = own * width * halves
    part = rows // width
    sites = part // ORB
    each = part // PIECES
    group = sites // PIECES
    near = screened.shape[0]
    here = near * width
    targets = kmap[:, 0]
    order = column_order(basis)

    sent = prepare(screened, order, width, PIECES)
    w = [lax.all_to_all(x, "kl", split_axis=0, concat_axis=0, tiled=True) for x in sent]

    green = jnp.dot(
        green_irr.reshape(own * 2 * rows, basis), order, preferred_element_type=jnp.float32
    ).astype(jnp.bfloat16)
    green = green.reshape(own, 2, width, part, basis).transpose(2, 0, 1, 3, 4)
    green = jnp.concatenate([green] * halves, axis=0)
    green = lax.all_to_all(green, both, split_axis=0, concat_axis=0, tiled=True)
    green = green.reshape(wedges, 2, sites, ORB, basis).transpose(2, 0, 3, 1, 4)
    green = green.reshape(sites, wedges * ORB, 2 * basis)

    cos_t, sin_t = phase_tables(zone)
    first_r = lax.axis_index("kh") * here
    forth = jnp.concatenate([cos_t, -sin_t], axis=1)
    forth = lax.dynamic_slice_in_dim(forth, first_r, here, 0)
    back_t = jnp.concatenate([cos_t, -sin_t], axis=0)
    back_t = lax.dynamic_slice_in_dim(back_t, first_r, here, 1)
    source, signs = decode(rotation)
    orbital = jnp.arange(ORB, dtype=jnp.int32)
    place = source - (jnp.arange(basis, dtype=jnp.int32) // ORB * ORB)[None, :]
    place = place.reshape(zone, atoms, ORB).transpose(2, 0, 1)
    sign = signs.reshape(zone, atoms, ORB).transpose(2, 0, 1)
    coef = (place[:, None] == orbital[None, :, None, None]).astype(jnp.bfloat16) * sign[:, None]

    first = lax.axis_index("ba") * rows // ORB + lax.axis_index("kl") * sites
    row_place = lax.dynamic_slice_in_dim(place, first, sites, 2).transpose(2, 0, 1)
    row_sign = lax.dynamic_slice_in_dim(sign, first, sites, 2).transpose(2, 0, 1)
    code = targets[None, None, :] * ORB + row_place
    hit = jnp.arange(wedges * ORB, dtype=jnp.int32)
    code = code.reshape(sites, ORB * zone)
    row_sign = row_sign.reshape(sites, ORB * zone)
    select = (code[:, :, None] == hit[None, None, :]).astype(jnp.bfloat16) * row_sign[:, :, None]
    back = (code[:, None, :] == hit[None, :, None]).astype(jnp.bfloat16) * row_sign[:, None, :]
    counts = jnp.sum(
        (targets[None, :] == (hit // ORB)[:, None]).astype(jnp.float32), axis=1, keepdims=True
    )

    whole = lambda shape: pl.BlockSpec(shape, lambda i: (0,) * len(shape))
    params = pltpu.CompilerParams(vmem_limit_bytes=40 << 20)
    cost = pl.CostEstimate(flops=20000000000, bytes_accessed=12 << 20, transcendentals=0)
    green_r = pl.pallas_call(
        unfold_kernel,
        grid=(sites,),
        in_specs=[
            pl.BlockSpec((1, ORB * zone, wedges * ORB), lambda i: (i, 0, 0)),
            pl.BlockSpec((1, wedges * ORB, 2 * basis), lambda i: (i, 0, 0)),
            whole(coef.shape),
            whole(forth.shape),
        ],
        out_specs=pl.BlockSpec((ORB, here, basis), lambda i: (i, 0, 0)),
        out_shape=jax.ShapeDtypeStruct((part, here, basis), jnp.bfloat16),
        scratch_shapes=[
            pltpu.VMEM((ORB * zone, 2 * basis), jnp.bfloat16),
            pltpu.VMEM((ORB, 2 * zone, basis), jnp.bfloat16),
        ],
        compiler_params=params,
        cost_estimate=cost,
    )(select, green, coef, forth)

    outs = []
    for piece in range(PIECES):
        skip = piece * group
        folded = pl.pallas_call(
            fold_kernel,
            grid=(group,),
            in_specs=[
                pl.BlockSpec((1, wedges * ORB, ORB * zone), lambda i, s=skip: (i + s, 0, 0)),
                whole((wedges * ORB, 1)),
                pl.BlockSpec((ORB, here, basis), lambda i, s=skip: (i + s, 0, 0)),
                pl.BlockSpec((width, ORB, near, basis), lambda i: (0, i, 0, 0)),
                whole(coef.shape),
                whole(back_t.shape),
            ],
            out_specs=pl.BlockSpec((1, wedges * ORB, 2 * basis), lambda i: (i, 0, 0)),
            out_shape=jax.ShapeDtypeStruct((group, wedges * ORB, 2 * basis), jnp.bfloat16),
            scratch_shapes=[
                pltpu.VMEM((ORB, 2 * zone, basis), jnp.bfloat16),
                pltpu.VMEM((ORB * zone, 2 * basis), jnp.bfloat16),
            ],
            compiler_params=params,
            cost_estimate=cost,
        )(back, counts, green_r, w[piece], coef, back_t)
        folded = folded.reshape(group, wedges, ORB, 2, basis).transpose(1, 3, 0, 2, 4)
        folded = folded.reshape(width * halves, own, 2, each, basis)
        folded = lax.all_to_all(folded, both, split_axis=0, concat_axis=0, tiled=True)
        folded = folded.reshape(halves, width * own * 2 * each, basis)
        out = sum(
            lax.dot_general(
                folded[h], order, (((1,), (1,)), ((), ())), preferred_element_type=jnp.float32
            )
            for h in range(halves)
        )
        outs.append(out.reshape(width, own, 2, each, basis))
    out = jnp.stack(outs, axis=1).transpose(2, 3, 0, 1, 4, 5)
    return out.reshape(own, 2, rows, basis)


def solution(mesh):
    sizes = mesh.shape
    width, lines = sizes["ka"], sizes["ba"]
    columns = (P("ka", None, "ba", None), P("ka", "ba", None), P(), P())

    def run(green_irr, screened, kmap, rotation):
        rows = green_irr.shape[2] // lines
        near = screened.shape[0] // width
        parts = width // HALVES
        if width % HALVES or rows % (parts * ORB * PIECES) or rows // parts % 16 or near % 16:
            return jax.shard_map(
                per_device_columns,
                mesh=mesh,
                in_specs=columns,
                out_specs=P("ka", None, "ba", None),
                check_vma=False,
            )(green_irr, screened, kmap, rotation)
        finer = Mesh(mesh.devices.reshape(HALVES, parts, lines), ("kh", "kl", "ba"))
        both = ("kh", "kl")
        placed = (P(both, None, "ba", None), P(both, "ba", None), P(), P())
        return jax.shard_map(
            per_device_rows,
            mesh=finer,
            in_specs=placed,
            out_specs=P(both, None, "ba", None),
            check_vma=False,
        )(green_irr, screened, kmap, rotation)

    return run
```

```python
import math

import jax
import jax.numpy as jnp
from jax import lax
from jax.experimental import pallas as pl
from jax.experimental.pallas import tpu as pltpu
from jax.sharding import Mesh
from jax.sharding import PartitionSpec as P

KX = 8
KY = 4
KZ = 4


def decode(rotation):
    source = jnp.where(rotation >= 0, rotation, -1 - rotation)
    signs = jnp.where(rotation >= 0, 1.0, -1.0).astype(jnp.bfloat16)
    return (source, signs)


def phase_tables(count):
    index = jnp.arange(count, dtype=jnp.int32)
    first = index // (KY * KZ)
    second = index // KZ % KY
    third = index % KZ
    turns = first[:, None] * first[None, :] + second[:, None] * second[None, :] * (KX // KY)
    turns = (turns + third[:, None] * third[None, :] * (KX // KZ)) % KX
    angle = turns.astype(jnp.float32) * (2.0 * math.pi / KX)
    return (jnp.cos(angle).astype(jnp.bfloat16), jnp.sin(angle).astype(jnp.bfloat16))


def turn_tables(local_source, local_signs, width):
    places = jnp.arange(width, dtype=jnp.int32)
    same = (local_source[:, :, None] == places[None, None, :]).astype(jnp.bfloat16)
    return same * local_signs[:, :, None]


def turn_forward(block, row_turn, col_turn):
    half = jnp.einsum("kab,kcbd->kcad", row_turn, block, preferred_element_type=jnp.float32).astype(
        jnp.bfloat16
    )
    return jnp.einsum("kcad,ked->kcae", half, col_turn, preferred_element_type=jnp.float32).astype(
        jnp.bfloat16
    )


def turn_back(block, row_turn, col_turn):
    half = jnp.einsum("kab,kcad->kcbd", row_turn, block, preferred_element_type=jnp.float32).astype(
        jnp.bfloat16
    )
    return jnp.einsum("kcbd,kde->kcbe", half, col_turn, preferred_element_type=jnp.float32).astype(
        jnp.bfloat16
    )


def per_device_columns(green_irr, screened, kmap, rotation):
    width_ka = lax.axis_size("ka")
    place_ka = lax.axis_index("ka")
    place_ba = lax.axis_index("ba")
    zone = rotation.shape[0]
    basis = rotation.shape[1]
    rows = green_irr.shape[2]
    cols = basis // width_ka
    wedges = green_irr.shape[0] * width_ka
    row_start = place_ba * rows
    col_start = place_ka * cols
    targets = kmap[:, 0]
    source, signs = decode(rotation)
    cos_t, sin_t = phase_tables(zone)
    counts = jnp.sum(
        (targets[:, None] == jnp.arange(wedges, dtype=jnp.int32)[None, :]).astype(jnp.float32),
        axis=0,
    )
    src_rows = lax.dynamic_slice_in_dim(source, row_start, rows, 1) - row_start
    sgn_rows = lax.dynamic_slice_in_dim(signs, row_start, rows, 1)
    moved = lax.all_to_all(green_irr, "ka", split_axis=3, concat_axis=0, tiled=True)
    src_cols = lax.dynamic_slice_in_dim(source, col_start, cols, 1) - col_start
    sgn_cols = lax.dynamic_slice_in_dim(signs, col_start, cols, 1)
    row_turn = turn_tables(src_rows, sgn_rows, rows)
    col_turn = turn_tables(src_cols, sgn_cols, cols)
    pick = (targets[:, None] == jnp.arange(wedges, dtype=jnp.int32)[None, :]).astype(jnp.bfloat16)
    selected = jnp.einsum("kn,ncab->kcab", pick, moved, preferred_element_type=jnp.float32).astype(
        jnp.bfloat16
    )
    green_k = turn_forward(selected, row_turn, col_turn)
    flat = green_k.reshape(zone, 2, rows * cols)
    green_r = (
        (
            jnp.dot(cos_t, flat[:, 0], preferred_element_type=jnp.float32)
            - jnp.dot(sin_t, flat[:, 1], preferred_element_type=jnp.float32)
        )
        * (1.0 / zone)
    ).astype(jnp.bfloat16)
    at_lattice = lax.all_to_all(
        green_r.reshape(zone, rows, cols), "ka", split_axis=0, concat_axis=2, tiled=True
    )
    product = (-(at_lattice.astype(jnp.float32) * screened.astype(jnp.float32))).astype(
        jnp.bfloat16
    )
    sigma_r = lax.all_to_all(product, "ka", split_axis=2, concat_axis=0, tiled=True).reshape(
        zone, rows * cols
    )
    real_k = jnp.dot(cos_t, sigma_r, preferred_element_type=jnp.float32).astype(jnp.bfloat16)
    imag_k = (-jnp.dot(sin_t, sigma_r, preferred_element_type=jnp.float32)).astype(jnp.bfloat16)
    sigma_k = jnp.stack([real_k, imag_k], axis=1).reshape(zone, 2, rows, cols)
    turned = turn_back(sigma_k, row_turn, col_turn)
    hit = (targets[None, :] == jnp.arange(wedges, dtype=jnp.int32)[:, None]).astype(jnp.bfloat16)
    folded = jnp.einsum("ik,kcab->icab", hit, turned, preferred_element_type=jnp.float32)
    folded = folded / counts[:, None, None, None]
    return lax.all_to_all(
        folded.astype(jnp.bfloat16), "ka", split_axis=0, concat_axis=3, tiled=True
    ).astype(folded.dtype)


ORB = 6


def column_order(basis):
    atoms = basis // ORB
    place = jnp.arange(basis, dtype=jnp.int32)
    moved = (place % ORB) * atoms + place // ORB
    return (moved[:, None] == place[None, :]).astype(jnp.bfloat16)


def prepare_kernel(swap_ref, order_ref, w_ref, *out_refs):
    count, rows, basis = w_ref.shape
    step = swap_ref.shape[0] // count
    each = rows // len(out_refs)
    for start in range(0, rows, step):
        block = w_ref[:, start : start + step, :].reshape(count * step, basis)
        turned = jnp.dot(swap_ref[...], block, preferred_element_type=jnp.float32)
        out = jnp.dot(
            turned.astype(jnp.bfloat16), order_ref[...], preferred_element_type=jnp.float32
        ).astype(jnp.bfloat16)
        out = out.reshape(step, count, basis)
        for row in range(start, start + step):
            out_refs[row // each][0, row % each] = out[row - start]


def prepare(screened, order, width, pieces, step=16):
    count, rows, basis = screened.shape
    part = rows // width
    each = part // pieces
    place = jnp.arange(count * step, dtype=jnp.int32)
    origin = (place % count) * step + place // count
    swap = (origin[:, None] == place[None, :]).astype(jnp.bfloat16)
    return pl.pallas_call(
        prepare_kernel,
        grid=(width,),
        in_specs=[
            pl.BlockSpec((count * step, count * step), lambda i: (0, 0)),
            pl.BlockSpec((basis, basis), lambda i: (0, 0)),
            pl.BlockSpec((count, part, basis), lambda i: (0, i, 0)),
        ],
        out_specs=[pl.BlockSpec((1, each, count, basis), lambda i: (i, 0, 0, 0))] * pieces,
        out_shape=[jax.ShapeDtypeStruct((width, each, count, basis), jnp.bfloat16)] * pieces,
        compiler_params=pltpu.CompilerParams(vmem_limit_bytes=24 << 20),
        cost_estimate=pl.CostEstimate(
            flops=4800000000, bytes_accessed=4 * count * rows * basis, transcendentals=0
        ),
    )(swap, order, screened)


def turn_columns(coef_ref, src, dst, zone, atoms, back):
    def chunk(step, carry):
        at = pl.ds(pl.multiple_of(step * 16, 16), 16)
        coef = [[coef_ref[o, p, at, :] for p in range(ORB)] for o in range(ORB)]
        for oa in range(ORB):
            for c in range(2):
                given = [src(oa, c, p, step) for p in range(ORB)]
                for o in range(ORB):
                    total = None
                    for p in range(ORB):
                        term = (coef[p][o] if back else coef[o][p]) * given[p]
                        total = term if total is None else total + term
                    dst(oa, c, o, step, total)
        return carry

    lax.fori_loop(0, zone // 16, chunk, 0)


def fill_coef(code_ref, coef_ref):
    atoms = coef_ref.shape[3]
    for o in range(ORB):
        code = code_ref[:, o * atoms : (o + 1) * atoms].astype(jnp.float32)
        sign = jnp.where(code < 0, -1.0, 1.0)
        for p in range(ORB):
            coef_ref[o, p] = jnp.where(jnp.abs(code) == p + 1.0, sign, 0.0).astype(jnp.bfloat16)


def row_select(code, count):
    place = lax.broadcasted_iota(jnp.int32, (count, code.shape[1]), 0).astype(jnp.float32) + 1.0
    sign = jnp.where(code < 0, -1.0, 1.0)
    return jnp.where(place == jnp.abs(code), sign, 0.0).astype(jnp.bfloat16)


def unfold_kernel(rows_ref, green_ref, code_ref, phase_ref, out_ref, coef_ref, half, full):
    zone = phase_ref.shape[1] // 2
    basis = out_ref.shape[2]
    atoms = basis // ORB
    count = green_ref.shape[1]

    @pl.when(pl.program_id(0) == 0)
    def _():
        fill_coef(code_ref, coef_ref)

    select = jnp.concatenate(
        [row_select(rows_ref[0, oa : oa + 1, :], count) for oa in range(ORB)], axis=1
    )
    half[...] = lax.dot_general(
        select, green_ref[0], (((0,), (0,)), ((), ())), preferred_element_type=jnp.float32
    ).astype(jnp.bfloat16)

    def read(oa, c, p, step):
        at = pl.ds(pl.multiple_of(oa * zone + step * 16, 16), 16)
        return half[at, c * basis + p * atoms : c * basis + (p + 1) * atoms]

    def write(oa, c, o, step, value):
        at = pl.ds(pl.multiple_of(c * zone + step * 16, 16), 16)
        full[oa, at, o * atoms : (o + 1) * atoms] = value

    turn_columns(coef_ref, read, write, zone, atoms, False)
    for oa in range(ORB):
        sums = jnp.dot(phase_ref[...], full[oa], preferred_element_type=jnp.float32)
        out_ref[oa] = (sums * (1.0 / zone)).astype(jnp.bfloat16)


def fold_kernel(
    rows_ref, target_ref, green_ref, w_ref, code_ref, phase_ref, out_ref, coef_ref, full, half
):
    near = phase_ref.shape[1]
    zone = phase_ref.shape[0] // 2
    basis = green_ref.shape[2]
    atoms = basis // ORB
    count = out_ref.shape[1]

    @pl.when(pl.program_id(0) == 0)
    def _():
        fill_coef(code_ref, coef_ref)

    for oa in range(ORB):
        w = w_ref[:, oa].reshape(near, basis)
        sigma = (-(green_ref[oa].astype(jnp.float32) * w.astype(jnp.float32))).astype(jnp.bfloat16)
        full[oa] = jnp.dot(phase_ref[...], sigma, preferred_element_type=jnp.float32).astype(
            jnp.bfloat16
        )

    def read(oa, c, p, step):
        at = pl.ds(pl.multiple_of(c * zone + step * 16, 16), 16)
        return full[oa, at, p * atoms : (p + 1) * atoms]

    def write(oa, c, o, step, value):
        at = pl.ds(pl.multiple_of(oa * zone + step * 16, 16), 16)
        half[at, c * basis + o * atoms : c * basis + (o + 1) * atoms] = value

    turn_columns(coef_ref, read, write, zone, atoms, True)
    select = jnp.concatenate(
        [row_select(rows_ref[0, oa : oa + 1, :], count) for oa in range(ORB)], axis=1
    )
    sums = jnp.dot(select, half[...], preferred_element_type=jnp.float32)
    point = lax.broadcasted_iota(jnp.int32, (count, zone), 0) // ORB
    named = jnp.where(point == target_ref[...], 1.0, 0.0)
    out_ref[0] = (sums / jnp.sum(named, axis=1, keepdims=True)).astype(jnp.bfloat16)


PIECES = 2
HALVES = 2


def per_device_rows(green_irr, screened, kmap, rotation):
    halves = lax.axis_size("kh")
    width = lax.axis_size("kl")
    both = ("kh", "kl")
    zone, basis = rotation.shape
    atoms = basis // ORB
    own, _, rows, _ = green_irr.shape
    wedges = own * width * halves
    part = rows // width
    sites = part // ORB
    each = part // PIECES
    group = sites // PIECES
    near = screened.shape[0]
    here = near * width
    order = column_order(basis)

    sent = prepare(screened, order, width, PIECES)
    w = [lax.all_to_all(x, "kl", split_axis=0, concat_axis=0, tiled=True) for x in sent]

    green = jnp.dot(
        green_irr.reshape(own * 2 * rows, basis), order, preferred_element_type=jnp.float32
    ).astype(jnp.bfloat16)
    green = green.reshape(own, 2, width, part, basis).transpose(2, 0, 1, 3, 4)
    green = jnp.concatenate([green] * halves, axis=0)
    green = lax.all_to_all(green, both, split_axis=0, concat_axis=0, tiled=True)
    green = green.reshape(wedges, 2, sites, ORB, basis).transpose(2, 0, 3, 1, 4)
    green = green.reshape(sites, wedges * ORB, 2 * basis)

    cos_t, sin_t = phase_tables(zone)
    first_r = lax.axis_index("kh") * here
    forth = jnp.concatenate([cos_t, -sin_t], axis=1)
    forth = lax.dynamic_slice_in_dim(forth, first_r, here, 0)
    back_t = jnp.concatenate([cos_t, -sin_t], axis=0)
    back_t = lax.dynamic_slice_in_dim(back_t, first_r, here, 1)

    source = jnp.where(rotation >= 0, rotation, -1 - rotation)
    place = source - (jnp.arange(basis, dtype=jnp.int32) // ORB * ORB)[None, :] + 1
    code = jnp.where(rotation >= 0, place, -place).astype(jnp.bfloat16)
    code = jnp.dot(code, order, preferred_element_type=jnp.float32).astype(jnp.bfloat16)
    first = lax.axis_index("ba") * rows + lax.axis_index("kl") * part
    row_place = lax.dynamic_slice_in_dim(place, first, part, 1) + kmap * ORB
    row_turn = lax.dynamic_slice_in_dim(rotation, first, part, 1)
    row_code = jnp.where(row_turn >= 0, row_place, -row_place).astype(jnp.float32)
    row_code = row_code.T.reshape(sites, ORB, zone)
    targets = kmap.reshape(1, zone)

    whole = lambda shape: pl.BlockSpec(shape, lambda i: (0,) * len(shape))
    params = pltpu.CompilerParams(vmem_limit_bytes=40 << 20)
    cost = pl.CostEstimate(flops=20000000000, bytes_accessed=12 << 20, transcendentals=0)
    green_r = pl.pallas_call(
        unfold_kernel,
        grid=(sites,),
        in_specs=[
            pl.BlockSpec((1, ORB, zone), lambda i: (i, 0, 0)),
            pl.BlockSpec((1, wedges * ORB, 2 * basis), lambda i: (i, 0, 0)),
            whole(code.shape),
            whole(forth.shape),
        ],
        out_specs=pl.BlockSpec((ORB, here, basis), lambda i: (i, 0, 0)),
        out_shape=jax.ShapeDtypeStruct((part, here, basis), jnp.bfloat16),
        scratch_shapes=[
            pltpu.VMEM((ORB, ORB, zone, atoms), jnp.bfloat16),
            pltpu.VMEM((ORB * zone, 2 * basis), jnp.bfloat16),
            pltpu.VMEM((ORB, 2 * zone, basis), jnp.bfloat16),
        ],
        compiler_params=params,
        cost_estimate=cost,
    )(row_code, green, code, forth)

    outs = []
    for piece in range(PIECES):
        skip = piece * group
        folded = pl.pallas_call(
            fold_kernel,
            grid=(group,),
            in_specs=[
                pl.BlockSpec((1, ORB, zone), lambda i, s=skip: (i + s, 0, 0)),
                whole((1, zone)),
                pl.BlockSpec((ORB, here, basis), lambda i, s=skip: (i + s, 0, 0)),
                pl.BlockSpec((width, ORB, near, basis), lambda i: (0, i, 0, 0)),
                whole(code.shape),
                whole(back_t.shape),
            ],
            out_specs=pl.BlockSpec((1, wedges * ORB, 2 * basis), lambda i: (i, 0, 0)),
            out_shape=jax.ShapeDtypeStruct((group, wedges * ORB, 2 * basis), jnp.bfloat16),
            scratch_shapes=[
            pltpu.VMEM((ORB, ORB, zone, atoms), jnp.bfloat16),
                pltpu.VMEM((ORB, 2 * zone, basis), jnp.bfloat16),
                pltpu.VMEM((ORB * zone, 2 * basis), jnp.bfloat16),
            ],
            compiler_params=params,
            cost_estimate=cost,
        )(row_code, targets, green_r, w[piece], code, back_t)
        folded = folded.reshape(group, wedges, ORB, 2, basis).transpose(1, 3, 0, 2, 4)
        folded = folded.reshape(width * halves, own, 2, each, basis)
        folded = lax.all_to_all(folded, both, split_axis=0, concat_axis=0, tiled=True)
        folded = folded.reshape(halves, width * own * 2 * each, basis)
        out = sum(
            lax.dot_general(
                folded[h], order, (((1,), (1,)), ((), ())), preferred_element_type=jnp.float32
            )
            for h in range(halves)
        )
        outs.append(out.reshape(width, own, 2, each, basis))
    out = jnp.stack(outs, axis=1).transpose(2, 3, 0, 1, 4, 5)
    return out.reshape(own, 2, rows, basis)


def solution(mesh):
    sizes = mesh.shape
    width, lines = sizes["ka"], sizes["ba"]
    columns = (P("ka", None, "ba", None), P("ka", "ba", None), P(), P())

    def run(green_irr, screened, kmap, rotation):
        rows = green_irr.shape[2] // lines
        near = screened.shape[0] // width
        parts = width // HALVES
        if width % HALVES or rows % (parts * ORB * PIECES) or rows // parts % 16 or near % 16:
            return jax.shard_map(
                per_device_columns,
                mesh=mesh,
                in_specs=columns,
                out_specs=P("ka", None, "ba", None),
                check_vma=False,
            )(green_irr, screened, kmap, rotation)
        finer = Mesh(mesh.devices.reshape(HALVES, parts, lines), ("kh", "kl", "ba"))
        both = ("kh", "kl")
        placed = (P(both, None, "ba", None), P(both, "ba", None), P(), P())
        return jax.shard_map(
            per_device_rows,
            mesh=finer,
            in_specs=placed,
            out_specs=P(both, None, "ba", None),
            check_vma=False,
        )(green_irr, screened, kmap, rotation)

    return run
```

```python
import functools
import math

import jax
import jax.numpy as jnp
from jax import lax
from jax.experimental import pallas as pl
from jax.experimental.pallas import tpu as pltpu
from jax.sharding import Mesh
from jax.sharding import PartitionSpec as P

KX = 8
KY = 4
KZ = 4


def decode(rotation):
    source = jnp.where(rotation >= 0, rotation, -1 - rotation)
    signs = jnp.where(rotation >= 0, 1.0, -1.0).astype(jnp.bfloat16)
    return (source, signs)


def phase_tables(count):
    index = jnp.arange(count, dtype=jnp.int32)
    first = index // (KY * KZ)
    second = index // KZ % KY
    third = index % KZ
    turns = first[:, None] * first[None, :] + second[:, None] * second[None, :] * (KX // KY)
    turns = (turns + third[:, None] * third[None, :] * (KX // KZ)) % KX
    angle = turns.astype(jnp.float32) * (2.0 * math.pi / KX)
    return (jnp.cos(angle).astype(jnp.bfloat16), jnp.sin(angle).astype(jnp.bfloat16))


def turn_tables(local_source, local_signs, width):
    places = jnp.arange(width, dtype=jnp.int32)
    same = (local_source[:, :, None] == places[None, None, :]).astype(jnp.bfloat16)
    return same * local_signs[:, :, None]


def turn_forward(block, row_turn, col_turn):
    half = jnp.einsum("kab,kcbd->kcad", row_turn, block, preferred_element_type=jnp.float32).astype(
        jnp.bfloat16
    )
    return jnp.einsum("kcad,ked->kcae", half, col_turn, preferred_element_type=jnp.float32).astype(
        jnp.bfloat16
    )


def turn_back(block, row_turn, col_turn):
    half = jnp.einsum("kab,kcad->kcbd", row_turn, block, preferred_element_type=jnp.float32).astype(
        jnp.bfloat16
    )
    return jnp.einsum("kcbd,kde->kcbe", half, col_turn, preferred_element_type=jnp.float32).astype(
        jnp.bfloat16
    )


def per_device_columns(green_irr, screened, kmap, rotation):
    width_ka = lax.axis_size("ka")
    place_ka = lax.axis_index("ka")
    place_ba = lax.axis_index("ba")
    zone = rotation.shape[0]
    basis = rotation.shape[1]
    rows = green_irr.shape[2]
    cols = basis // width_ka
    wedges = green_irr.shape[0] * width_ka
    row_start = place_ba * rows
    col_start = place_ka * cols
    targets = kmap[:, 0]
    source, signs = decode(rotation)
    cos_t, sin_t = phase_tables(zone)
    counts = jnp.sum(
        (targets[:, None] == jnp.arange(wedges, dtype=jnp.int32)[None, :]).astype(jnp.float32),
        axis=0,
    )
    src_rows = lax.dynamic_slice_in_dim(source, row_start, rows, 1) - row_start
    sgn_rows = lax.dynamic_slice_in_dim(signs, row_start, rows, 1)
    moved = lax.all_to_all(green_irr, "ka", split_axis=3, concat_axis=0, tiled=True)
    src_cols = lax.dynamic_slice_in_dim(source, col_start, cols, 1) - col_start
    sgn_cols = lax.dynamic_slice_in_dim(signs, col_start, cols, 1)
    row_turn = turn_tables(src_rows, sgn_rows, rows)
    col_turn = turn_tables(src_cols, sgn_cols, cols)
    pick = (targets[:, None] == jnp.arange(wedges, dtype=jnp.int32)[None, :]).astype(jnp.bfloat16)
    selected = jnp.einsum("kn,ncab->kcab", pick, moved, preferred_element_type=jnp.float32).astype(
        jnp.bfloat16
    )
    green_k = turn_forward(selected, row_turn, col_turn)
    flat = green_k.reshape(zone, 2, rows * cols)
    green_r = (
        (
            jnp.dot(cos_t, flat[:, 0], preferred_element_type=jnp.float32)
            - jnp.dot(sin_t, flat[:, 1], preferred_element_type=jnp.float32)
        )
        * (1.0 / zone)
    ).astype(jnp.bfloat16)
    at_lattice = lax.all_to_all(
        green_r.reshape(zone, rows, cols), "ka", split_axis=0, concat_axis=2, tiled=True
    )
    product = (-(at_lattice.astype(jnp.float32) * screened.astype(jnp.float32))).astype(
        jnp.bfloat16
    )
    sigma_r = lax.all_to_all(product, "ka", split_axis=2, concat_axis=0, tiled=True).reshape(
        zone, rows * cols
    )
    real_k = jnp.dot(cos_t, sigma_r, preferred_element_type=jnp.float32).astype(jnp.bfloat16)
    imag_k = (-jnp.dot(sin_t, sigma_r, preferred_element_type=jnp.float32)).astype(jnp.bfloat16)
    sigma_k = jnp.stack([real_k, imag_k], axis=1).reshape(zone, 2, rows, cols)
    turned = turn_back(sigma_k, row_turn, col_turn)
    hit = (targets[None, :] == jnp.arange(wedges, dtype=jnp.int32)[:, None]).astype(jnp.bfloat16)
    folded = jnp.einsum("ik,kcab->icab", hit, turned, preferred_element_type=jnp.float32)
    folded = folded / counts[:, None, None, None]
    return lax.all_to_all(
        folded.astype(jnp.bfloat16), "ka", split_axis=0, concat_axis=3, tiled=True
    ).astype(folded.dtype)


ORB = 6


def column_order(basis):
    atoms = basis // ORB
    place = jnp.arange(basis, dtype=jnp.int32)
    moved = (place % ORB) * atoms + place // ORB
    return (moved[:, None] == place[None, :]).astype(jnp.bfloat16)


def turn_columns(coef_ref, parts, src, dst, zone, back):
    def chunk(step, carry):
        at = pl.ds(pl.multiple_of(step * 16, 16), 16)
        coef = [[coef_ref[o, p, at, :] for p in range(ORB)] for o in range(ORB)]
        for oa in range(ORB):
            for c in parts:
                given = [src(oa, c, p, step) for p in range(ORB)]
                for o in range(ORB):
                    total = None
                    for p in range(ORB):
                        term = (coef[p][o] if back else coef[o][p]) * given[p]
                        total = term if total is None else total + term
                    dst(oa, c, o, step, total)
        return carry

    lax.fori_loop(0, zone // 16, chunk, 0)


def fill_coef(code_ref, coef_ref):
    atoms = coef_ref.shape[3]
    for o in range(ORB):
        code = code_ref[:, o * atoms : (o + 1) * atoms].astype(jnp.float32)
        sign = jnp.where(code < 0, -1.0, 1.0)
        for p in range(ORB):
            coef_ref[o, p] = jnp.where(jnp.abs(code) == p + 1.0, sign, 0.0).astype(jnp.bfloat16)


def row_select(code, count):
    place = lax.broadcasted_iota(jnp.int32, (count, code.shape[1]), 0).astype(jnp.float32) + 1.0
    sign = jnp.where(code < 0, -1.0, 1.0)
    return jnp.where(place == jnp.abs(code), sign, 0.0).astype(jnp.bfloat16)


def site_select(rows_ref, site, count):
    return jnp.concatenate(
        [row_select(rows_ref[site, oa : oa + 1, :], count) for oa in range(ORB)], axis=1
    )


def kernel(
    halves, width, swap_ref, order_ref, site_ref, green_ref, w_ref, rows_ref, target_ref,
    code_ref, forth_ref, back_ref, out_ref,
    g_send, g_recv, g_all, w_send, w_recv, green_r, coef_ref, half, full, stage, o_send, o_recv,
    g_out, g_in, w_out, w_in, o_out, o_in,
):
    total = halves * width
    kh, kl = lax.axis_index("kh"), lax.axis_index("kl")
    me = kh * width + kl
    near, rows, basis = w_ref.shape
    zone = code_ref.shape[0]
    atoms = basis // ORB
    part = rows // width
    sites = part // ORB
    count = total * ORB
    step = swap_ref.shape[0] // near
    here = near * width
    f32, bf16 = jnp.float32, jnp.bfloat16

    def peer(off):
        other = lax.rem(me + off, total)
        return other, {"kh": other // width, "kl": lax.rem(other, width)}

    barrier = pltpu.get_barrier_semaphore()
    for off in range(1, total):
        pl.semaphore_signal(
            barrier, inc=1, device_id=peer(off)[1], device_id_type=pl.DeviceIdType.MESH
        )
    pl.semaphore_wait(barrier, total - 1)

    def green_copy(off):
        other, where = peer(off)
        return pltpu.make_async_remote_copy(
            src_ref=g_send.at[lax.rem(other, width)],
            dst_ref=g_recv.at[me],
            send_sem=g_out.at[off - 1],
            recv_sem=g_in.at[off - 1],
            device_id=where,
            device_id_type=pl.DeviceIdType.MESH,
        )

    for c in range(2):
        moved = jnp.dot(
            green_ref[c * rows : (c + 1) * rows, :], order_ref[...], preferred_element_type=f32
        ).astype(bf16)
        for k in range(width):
            g_send[k, c] = moved[k * part : (k + 1) * part]
    for off in range(1, total):
        green_copy(off).start()
    g_recv[me] = g_send[kl]

    blocks = part // step

    def w_place(t):
        off = 1 + lax.rem(t, width - 1)
        return lax.rem(kl + off, width), t // (width - 1)

    def w_copy(t):
        to, b = w_place(t)
        at = pl.ds(b * step, step)
        return pltpu.make_async_remote_copy(
            src_ref=w_send.at[to, at],
            dst_ref=w_recv.at[kl, at],
            send_sem=w_out.at[t],
            recv_sem=w_in.at[t],
            device_id={"kh": kh, "kl": to},
            device_id_type=pl.DeviceIdType.MESH,
        )

    def prepared(to, b):
        at = pl.ds(pl.multiple_of(to * part + b * step, step), step)
        block = w_ref[:, at, :].reshape(near * step, basis)
        turned = jnp.dot(swap_ref[...], block, preferred_element_type=f32).astype(bf16)
        out = jnp.dot(turned, order_ref[...], preferred_element_type=f32).astype(bf16)
        return out.reshape(step, near, basis)

    def w_start(t, carry):
        to, b = w_place(t)
        w_send[to, pl.ds(b * step, step)] = prepared(to, b)
        w_copy(t).start()
        return carry

    lax.fori_loop(0, blocks * (width - 1), w_start, 0)

    def w_own(b, carry):
        w_recv[kl, pl.ds(b * step, step)] = prepared(kl, b)
        return carry

    lax.fori_loop(0, blocks, w_own, 0)
    fill_coef(code_ref, coef_ref)

    for off in range(1, total):
        green_copy(off).wait_recv()
    for c in range(2):
        given = g_recv[:, c].reshape(total * part, basis)
        g_all[:, :, c * basis : (c + 1) * basis] = (
            lax.dot_general(
                site_ref[...], given, (((0,), (0,)), ((), ())), preferred_element_type=f32
            )
            .astype(bf16)
            .reshape(sites, count, basis)
        )

    def unfold(site, carry):
        half[...] = lax.dot_general(
            site_select(rows_ref, site, count),
            g_all[site],
            (((0,), (0,)), ((), ())),
            preferred_element_type=f32,
        ).astype(bf16)

        def read(oa, c, p, at):
            at = pl.ds(pl.multiple_of(oa * zone + at * 16, 16), 16)
            return half[at, c * basis + p * atoms : c * basis + (p + 1) * atoms]

        def write(oa, c, o, at, value):
            at = pl.ds(pl.multiple_of(c * zone + at * 16, 16), 16)
            full[oa, at, o * atoms : (o + 1) * atoms] = value

        turn_columns(coef_ref, (0, 1), read, write, zone, False)
        for oa in range(ORB):
            sums = jnp.dot(forth_ref[...], full[oa], preferred_element_type=f32)
            green_r[site * ORB + oa] = (sums * (1.0 / zone)).astype(bf16)
        return carry

    lax.fori_loop(0, sites, unfold, 0)

    def w_arrived(t, carry):
        w_copy(t).wait_recv()
        return carry

    lax.fori_loop(0, blocks * (width - 1), w_arrived, 0)

    point = lax.broadcasted_iota(jnp.int32, (count, zone), 0) // ORB
    named = jnp.where(point == target_ref[...], 1.0, 0.0)
    counts = jnp.sum(named, axis=1, keepdims=True)

    def out_copy(off, c):
        other, where = peer(off)
        return pltpu.make_async_remote_copy(
            src_ref=o_send.at[other, c],
            dst_ref=o_recv.at[me, c],
            send_sem=o_out.at[c, off - 1],
            recv_sem=o_in.at[c, off - 1],
            device_id=where,
            device_id_type=pl.DeviceIdType.MESH,
        )

    for c in range(2):

        def fold(site, carry, c=c):
            for oa in range(ORB):
                row = site * ORB + oa
                if c == 0:
                    w = w_recv[:, row].reshape(here, basis).astype(f32)
                    sigma = (-(green_r[row].astype(f32) * w)).astype(bf16)
                    green_r[row] = sigma
                else:
                    sigma = green_r[row]
                full[oa, 0:zone] = jnp.dot(
                    back_ref[c * zone : (c + 1) * zone, :], sigma, preferred_element_type=f32
                ).astype(bf16)

            def read(oa, c, p, at):
                at = pl.ds(pl.multiple_of(at * 16, 16), 16)
                return full[oa, at, p * atoms : (p + 1) * atoms]

            def write(oa, c, o, at, value):
                at = pl.ds(pl.multiple_of(oa * zone + at * 16, 16), 16)
                half[at, o * atoms : (o + 1) * atoms] = value

            turn_columns(coef_ref, (c,), read, write, zone, True)
            sums = jnp.dot(
                site_select(rows_ref, site, count), half[:, 0:basis], preferred_element_type=f32
            )
            stage[site] = (sums / counts).astype(bf16)
            return carry

        lax.fori_loop(0, sites, fold, 0)
        o_send[:, c] = (
            jnp.dot(
                site_ref[...], stage[...].reshape(sites * count, basis), preferred_element_type=f32
            )
            .astype(bf16)
            .reshape(total, part, basis)
        )
        for off in range(1, total):
            out_copy(off, c).start()
        o_recv[me, c] = o_send[me, c]

    for c in range(2):
        for off in range(1, total):
            out_copy(off, c).wait_recv()
        sums = None
        for h in range(halves):
            given = o_recv[h * width : (h + 1) * width, c].reshape(rows, basis)
            term = lax.dot_general(
                given, order_ref[...], (((1,), (1,)), ((), ())), preferred_element_type=f32
            )
            sums = term if sums is None else sums + term
        out_ref[c] = sums

    for off in range(1, total):
        green_copy(off).wait_send()
        for c in range(2):
            out_copy(off, c).wait_send()

    def w_sent(t, carry):
        w_copy(t).wait_send()
        return carry

    lax.fori_loop(0, blocks * (width - 1), w_sent, 0)


HALVES = 2
STEP = 16


def per_device_rows(green_irr, screened, kmap, rotation):
    halves = lax.axis_size("kh")
    width = lax.axis_size("kl")
    total = halves * width
    zone, basis = rotation.shape
    rows = green_irr.shape[2]
    part = rows // width
    sites = part // ORB
    near = screened.shape[0]
    here = near * width
    count = total * ORB
    order = column_order(basis)

    place = jnp.arange(near * STEP, dtype=jnp.int32)
    swap = ((place % near * STEP + place // near)[:, None] == place[None, :]).astype(jnp.bfloat16)
    place = jnp.arange(total * part, dtype=jnp.int32)
    origin = place % part // ORB * count + place // part * ORB + place % ORB
    site = (origin[:, None] == place[None, :]).astype(jnp.bfloat16)

    cos_t, sin_t = phase_tables(zone)
    first_r = lax.axis_index("kh") * here
    forth = jnp.concatenate([cos_t, -sin_t], axis=1)
    forth = lax.dynamic_slice_in_dim(forth, first_r, here, 0)
    back_t = jnp.concatenate([cos_t, -sin_t], axis=0)
    back_t = lax.dynamic_slice_in_dim(back_t, first_r, here, 1)

    source = jnp.where(rotation >= 0, rotation, -1 - rotation)
    place = source - (jnp.arange(basis, dtype=jnp.int32) // ORB * ORB)[None, :] + 1
    code = jnp.where(rotation >= 0, place, -place).astype(jnp.bfloat16)
    code = jnp.dot(code, order, preferred_element_type=jnp.float32).astype(jnp.bfloat16)
    first = lax.axis_index("ba") * rows + lax.axis_index("kl") * part
    row_place = lax.dynamic_slice_in_dim(place, first, part, 1) + kmap * ORB
    row_turn = lax.dynamic_slice_in_dim(rotation, first, part, 1)
    row_code = jnp.where(row_turn >= 0, row_place, -row_place).astype(jnp.float32)
    row_code = row_code.T.reshape(sites, ORB, zone)
    targets = kmap.reshape(1, zone)

    bf16 = jnp.bfloat16
    vmem = pl.BlockSpec(memory_space=pltpu.VMEM)
    copies = part // STEP * (width - 1)
    out = pl.pallas_call(
        functools.partial(kernel, halves, width),
        in_specs=[vmem] * 10,
        out_specs=vmem,
        out_shape=jax.ShapeDtypeStruct((2, rows, basis), jnp.float32),
        scratch_shapes=[
            pltpu.VMEM((width, 2, part, basis), bf16),
            pltpu.VMEM((total, 2, part, basis), bf16),
            pltpu.VMEM((sites, count, 2 * basis), bf16),
            pltpu.VMEM((width, part, near, basis), bf16),
            pltpu.VMEM((width, part, near, basis), bf16),
            pltpu.VMEM((part, here, basis), bf16),
            pltpu.VMEM((ORB, ORB, zone, basis // ORB), bf16),
            pltpu.VMEM((ORB * zone, 2 * basis), bf16),
            pltpu.VMEM((ORB, 2 * zone, basis), bf16),
            pltpu.VMEM((sites, count, basis), bf16),
            pltpu.VMEM((total, 2, part, basis), bf16),
            pltpu.VMEM((total, 2, part, basis), bf16),
            pltpu.SemaphoreType.DMA((total - 1,)),
            pltpu.SemaphoreType.DMA((total - 1,)),
            pltpu.SemaphoreType.DMA((copies,)),
            pltpu.SemaphoreType.DMA((copies,)),
            pltpu.SemaphoreType.DMA((2, total - 1)),
            pltpu.SemaphoreType.DMA((2, total - 1)),
        ],
        compiler_params=pltpu.CompilerParams(
            collective_id=0, has_side_effects=True, vmem_limit_bytes=52 << 20
        ),
        cost_estimate=pl.CostEstimate(
            flops=60000000000, bytes_accessed=12 << 20, transcendentals=0
        ),
    )(
        swap, order, site, green_irr.reshape(2 * rows, basis), screened, row_code, targets,
        code, forth, back_t,
    )
    return out.reshape(1, 2, rows, basis)


def solution(mesh):
    sizes = mesh.shape
    width, lines = sizes["ka"], sizes["ba"]
    columns = (P("ka", None, "ba", None), P("ka", "ba", None), P(), P())

    def run(green_irr, screened, kmap, rotation):
        rows = green_irr.shape[2] // lines
        near = screened.shape[0] // width
        parts = width // HALVES
        if green_irr.shape[0] != width or width % HALVES or rows % (parts * ORB * 8) or near % 16:
            return jax.shard_map(
                per_device_columns,
                mesh=mesh,
                in_specs=columns,
                out_specs=P("ka", None, "ba", None),
                check_vma=False,
            )(green_irr, screened, kmap, rotation)
        finer = Mesh(mesh.devices.reshape(HALVES, parts, lines), ("kh", "kl", "ba"))
        both = ("kh", "kl")
        placed = (P(both, None, "ba", None), P(both, "ba", None), P(), P())
        return jax.shard_map(
            per_device_rows,
            mesh=finer,
            in_specs=placed,
            out_specs=P(both, None, "ba", None),
            check_vma=False,
        )(green_irr, screened, kmap, rotation)

    return run
```

```python
import functools
import math

import jax
import jax.numpy as jnp
from jax import lax
from jax.experimental import pallas as pl
from jax.experimental.pallas import tpu as pltpu
from jax.sharding import Mesh
from jax.sharding import PartitionSpec as P

KX = 8
KY = 4
KZ = 4


def decode(rotation):
    source = jnp.where(rotation >= 0, rotation, -1 - rotation)
    signs = jnp.where(rotation >= 0, 1.0, -1.0).astype(jnp.bfloat16)
    return (source, signs)


def phase_tables(count):
    index = jnp.arange(count, dtype=jnp.int32)
    first = index // (KY * KZ)
    second = index // KZ % KY
    third = index % KZ
    turns = first[:, None] * first[None, :] + second[:, None] * second[None, :] * (KX // KY)
    turns = (turns + third[:, None] * third[None, :] * (KX // KZ)) % KX
    angle = turns.astype(jnp.float32) * (2.0 * math.pi / KX)
    return (jnp.cos(angle).astype(jnp.bfloat16), jnp.sin(angle).astype(jnp.bfloat16))


def turn_tables(local_source, local_signs, width):
    places = jnp.arange(width, dtype=jnp.int32)
    same = (local_source[:, :, None] == places[None, None, :]).astype(jnp.bfloat16)
    return same * local_signs[:, :, None]


def turn_forward(block, row_turn, col_turn):
    half = jnp.einsum("kab,kcbd->kcad", row_turn, block, preferred_element_type=jnp.float32).astype(
        jnp.bfloat16
    )
    return jnp.einsum("kcad,ked->kcae", half, col_turn, preferred_element_type=jnp.float32).astype(
        jnp.bfloat16
    )


def turn_back(block, row_turn, col_turn):
    half = jnp.einsum("kab,kcad->kcbd", row_turn, block, preferred_element_type=jnp.float32).astype(
        jnp.bfloat16
    )
    return jnp.einsum("kcbd,kde->kcbe", half, col_turn, preferred_element_type=jnp.float32).astype(
        jnp.bfloat16
    )


def per_device_columns(green_irr, screened, kmap, rotation):
    width_ka = lax.axis_size("ka")
    place_ka = lax.axis_index("ka")
    place_ba = lax.axis_index("ba")
    zone = rotation.shape[0]
    basis = rotation.shape[1]
    rows = green_irr.shape[2]
    cols = basis // width_ka
    wedges = green_irr.shape[0] * width_ka
    row_start = place_ba * rows
    col_start = place_ka * cols
    targets = kmap[:, 0]
    source, signs = decode(rotation)
    cos_t, sin_t = phase_tables(zone)
    counts = jnp.sum(
        (targets[:, None] == jnp.arange(wedges, dtype=jnp.int32)[None, :]).astype(jnp.float32),
        axis=0,
    )
    src_rows = lax.dynamic_slice_in_dim(source, row_start, rows, 1) - row_start
    sgn_rows = lax.dynamic_slice_in_dim(signs, row_start, rows, 1)
    moved = lax.all_to_all(green_irr, "ka", split_axis=3, concat_axis=0, tiled=True)
    src_cols = lax.dynamic_slice_in_dim(source, col_start, cols, 1) - col_start
    sgn_cols = lax.dynamic_slice_in_dim(signs, col_start, cols, 1)
    row_turn = turn_tables(src_rows, sgn_rows, rows)
    col_turn = turn_tables(src_cols, sgn_cols, cols)
    pick = (targets[:, None] == jnp.arange(wedges, dtype=jnp.int32)[None, :]).astype(jnp.bfloat16)
    selected = jnp.einsum("kn,ncab->kcab", pick, moved, preferred_element_type=jnp.float32).astype(
        jnp.bfloat16
    )
    green_k = turn_forward(selected, row_turn, col_turn)
    flat = green_k.reshape(zone, 2, rows * cols)
    green_r = (
        (
            jnp.dot(cos_t, flat[:, 0], preferred_element_type=jnp.float32)
            - jnp.dot(sin_t, flat[:, 1], preferred_element_type=jnp.float32)
        )
        * (1.0 / zone)
    ).astype(jnp.bfloat16)
    at_lattice = lax.all_to_all(
        green_r.reshape(zone, rows, cols), "ka", split_axis=0, concat_axis=2, tiled=True
    )
    product = (-(at_lattice.astype(jnp.float32) * screened.astype(jnp.float32))).astype(
        jnp.bfloat16
    )
    sigma_r = lax.all_to_all(product, "ka", split_axis=2, concat_axis=0, tiled=True).reshape(
        zone, rows * cols
    )
    real_k = jnp.dot(cos_t, sigma_r, preferred_element_type=jnp.float32).astype(jnp.bfloat16)
    imag_k = (-jnp.dot(sin_t, sigma_r, preferred_element_type=jnp.float32)).astype(jnp.bfloat16)
    sigma_k = jnp.stack([real_k, imag_k], axis=1).reshape(zone, 2, rows, cols)
    turned = turn_back(sigma_k, row_turn, col_turn)
    hit = (targets[None, :] == jnp.arange(wedges, dtype=jnp.int32)[:, None]).astype(jnp.bfloat16)
    folded = jnp.einsum("ik,kcab->icab", hit, turned, preferred_element_type=jnp.float32)
    folded = folded / counts[:, None, None, None]
    return lax.all_to_all(
        folded.astype(jnp.bfloat16), "ka", split_axis=0, concat_axis=3, tiled=True
    ).astype(folded.dtype)


ORB = 6


def column_order(basis):
    atoms = basis // ORB
    place = jnp.arange(basis, dtype=jnp.int32)
    moved = (place % ORB) * atoms + place // ORB
    return (moved[:, None] == place[None, :]).astype(jnp.bfloat16)


def turn_columns(coef_ref, parts, src, dst, zone, back):
    def chunk(step, carry):
        at = pl.ds(pl.multiple_of(step * 16, 16), 16)
        coef = [[coef_ref[o, p, at, :] for p in range(ORB)] for o in range(ORB)]
        for oa in range(ORB):
            for c in parts:
                given = [src(oa, c, p, step) for p in range(ORB)]
                for o in range(ORB):
                    total = None
                    for p in range(ORB):
                        term = (coef[p][o] if back else coef[o][p]) * given[p]
                        total = term if total is None else total + term
                    dst(oa, c, o, step, total)
        return carry

    lax.fori_loop(0, zone // 16, chunk, 0)


def fill_coef(code_ref, coef_ref):
    atoms = coef_ref.shape[3]
    for o in range(ORB):
        code = code_ref[:, o * atoms : (o + 1) * atoms].astype(jnp.float32)
        sign = jnp.where(code < 0, -1.0, 1.0)
        for p in range(ORB):
            coef_ref[o, p] = jnp.where(jnp.abs(code) == p + 1.0, sign, 0.0).astype(jnp.bfloat16)


def row_select(code, count):
    place = lax.broadcasted_iota(jnp.int32, (count, code.shape[1]), 0).astype(jnp.float32) + 1.0
    sign = jnp.where(code < 0, -1.0, 1.0)
    return jnp.where(place == jnp.abs(code), sign, 0.0).astype(jnp.bfloat16)


def site_select(rows_ref, site, count):
    return jnp.concatenate(
        [row_select(rows_ref[site, oa : oa + 1, :], count) for oa in range(ORB)], axis=1
    )


def kernel(
    halves, width, swap_ref, order_ref, site_ref, green_ref, w_ref, rows_ref, target_ref,
    code_ref, forth_ref, back_ref, out_ref,
    g_send, g_recv, g_all, w_send, w_recv, green_r, coef_ref, half, full, stage, o_send, o_recv,
    g_out, g_in, w_out, w_in, o_out, o_in,
):
    total = halves * width
    kh, kl = lax.axis_index("kh"), lax.axis_index("kl")
    me = kh * width + kl
    near, rows, basis = w_ref.shape
    zone = code_ref.shape[0]
    atoms = basis // ORB
    part = rows // width
    sites = part // ORB
    count = total * ORB
    step = swap_ref.shape[0] // near
    here = near * width
    f32, bf16 = jnp.float32, jnp.bfloat16

    def peer(off):
        other = lax.rem(me + off, total)
        return other, {"kh": other // width, "kl": lax.rem(other, width)}

    barrier = pltpu.get_barrier_semaphore()
    for off in range(1, total):
        pl.semaphore_signal(
            barrier, inc=1, device_id=peer(off)[1], device_id_type=pl.DeviceIdType.MESH
        )
    pl.semaphore_wait(barrier, total - 1)

    def green_copy(off):
        other, where = peer(off)
        return pltpu.make_async_remote_copy(
            src_ref=g_send.at[lax.rem(other, width)],
            dst_ref=g_recv.at[me],
            send_sem=g_out.at[off - 1],
            recv_sem=g_in.at[off - 1],
            device_id=where,
            device_id_type=pl.DeviceIdType.MESH,
        )

    for c in range(2):
        moved = jnp.dot(
            green_ref[c * rows : (c + 1) * rows, :], order_ref[...], preferred_element_type=f32
        ).astype(bf16)
        for k in range(width):
            g_send[k, c] = moved[k * part : (k + 1) * part]
    for off in range(1, total):
        green_copy(off).start()
    g_recv[me] = g_send[kl]

    blocks = part // step

    def w_place(t):
        off = 1 + lax.rem(t, width - 1)
        return lax.rem(kl + off, width), t // (width - 1)

    def w_copy(t):
        to, b = w_place(t)
        at = pl.ds(b * step, step)
        return pltpu.make_async_remote_copy(
            src_ref=w_send.at[to, at],
            dst_ref=w_recv.at[kl, at],
            send_sem=w_out.at[t],
            recv_sem=w_in.at[t],
            device_id={"kh": kh, "kl": to},
            device_id_type=pl.DeviceIdType.MESH,
        )

    def prepared(to, b):
        at = pl.ds(pl.multiple_of(to * part + b * step, step), step)
        block = w_ref[:, at, :].reshape(near * step, basis)
        turned = jnp.dot(swap_ref[...], block, preferred_element_type=f32).astype(bf16)
        out = jnp.dot(turned, order_ref[...], preferred_element_type=f32).astype(bf16)
        return out.reshape(step, near, basis)

    def w_start(t, carry):
        to, b = w_place(t)
        w_send[to, pl.ds(b * step, step)] = prepared(to, b)
        w_copy(t).start()
        return carry

    lax.fori_loop(0, blocks * (width - 1), w_start, 0)

    def w_own(b, carry):
        w_recv[kl, pl.ds(b * step, step)] = prepared(kl, b)
        return carry

    lax.fori_loop(0, blocks, w_own, 0)
    fill_coef(code_ref, coef_ref)

    for off in range(1, total):
        green_copy(off).wait_recv()
    for c in range(2):
        given = g_recv[:, c].reshape(total * part, basis)
        g_all[:, :, c * basis : (c + 1) * basis] = (
            lax.dot_general(
                site_ref[...], given, (((0,), (0,)), ((), ())), preferred_element_type=f32
            )
            .astype(bf16)
            .reshape(sites, count, basis)
        )

    def unfold(site, carry):
        half[...] = lax.dot_general(
            site_select(rows_ref, site, count),
            g_all[site],
            (((0,), (0,)), ((), ())),
            preferred_element_type=f32,
        ).astype(bf16)

        def read(oa, c, p, at):
            at = pl.ds(pl.multiple_of(oa * zone + at * 16, 16), 16)
            return half[at, c * basis + p * atoms : c * basis + (p + 1) * atoms]

        def write(oa, c, o, at, value):
            at = pl.ds(pl.multiple_of(c * zone + at * 16, 16), 16)
            full[oa, at, o * atoms : (o + 1) * atoms] = value

        turn_columns(coef_ref, (0, 1), read, write, zone, False)
        for oa in range(ORB):
            sums = jnp.dot(forth_ref[...], full[oa], preferred_element_type=f32)
            green_r[site * ORB + oa] = (sums * (1.0 / zone)).astype(bf16)
        return carry

    lax.fori_loop(0, sites, unfold, 0)

    def w_arrived(b):
        for t in range(b * (width - 1), (b + 1) * (width - 1)):
            w_copy(t).wait_recv()

    point = lax.broadcasted_iota(jnp.int32, (count, zone), 0) // ORB
    named = jnp.where(point == target_ref[...], 1.0, 0.0)
    counts = jnp.sum(named, axis=1, keepdims=True)

    def out_copy(off, c):
        other, where = peer(off)
        return pltpu.make_async_remote_copy(
            src_ref=o_send.at[other, c],
            dst_ref=o_recv.at[me, c],
            send_sem=o_out.at[c, off - 1],
            recv_sem=o_in.at[c, off - 1],
            device_id=where,
            device_id_type=pl.DeviceIdType.MESH,
        )

    def fold(c, site):
        for oa in range(ORB):
            row = site * ORB + oa
            if c == 0:
                w = w_recv[:, row].reshape(here, basis).astype(f32)
                sigma = (-(green_r[row].astype(f32) * w)).astype(bf16)
                green_r[row] = sigma
            else:
                sigma = green_r[row]
            full[oa, 0:zone] = jnp.dot(
                back_ref[c * zone : (c + 1) * zone, :], sigma, preferred_element_type=f32
            ).astype(bf16)

        def read(oa, c, p, at):
            at = pl.ds(pl.multiple_of(at * 16, 16), 16)
            return full[oa, at, p * atoms : (p + 1) * atoms]

        def write(oa, c, o, at, value):
            at = pl.ds(pl.multiple_of(oa * zone + at * 16, 16), 16)
            half[at, o * atoms : (o + 1) * atoms] = value

        turn_columns(coef_ref, (c,), read, write, zone, True)
        sums = jnp.dot(
            site_select(rows_ref, site, count), half[:, 0:basis], preferred_element_type=f32
        )
        stage[c, site] = (sums / counts).astype(bf16)

    starts = [b * step // ORB for b in range(blocks)]

    def fold_both(site, carry):
        for b in range(blocks - 1):
            pl.when(site == starts[b])(functools.partial(w_arrived, b))
        fold(0, site)
        fold(1, site)
        return carry

    lax.fori_loop(0, starts[-1], fold_both, 0)
    w_arrived(blocks - 1)
    for c in range(2):

        def fold_one(site, carry, c=c):
            fold(c, site)
            return carry

        lax.fori_loop(starts[-1], sites, fold_one, 0)
        o_send[:, c] = (
            jnp.dot(
                site_ref[...],
                stage[c].reshape(sites * count, basis),
                preferred_element_type=f32,
            )
            .astype(bf16)
            .reshape(total, part, basis)
        )
        for off in range(1, total):
            out_copy(off, c).start()
        o_recv[me, c] = o_send[me, c]

    for c in range(2):
        for off in range(1, total):
            out_copy(off, c).wait_recv()
        sums = None
        for h in range(halves):
            given = o_recv[h * width : (h + 1) * width, c].reshape(rows, basis)
            term = lax.dot_general(
                given, order_ref[...], (((1,), (1,)), ((), ())), preferred_element_type=f32
            )
            sums = term if sums is None else sums + term
        out_ref[c] = sums

    for off in range(1, total):
        green_copy(off).wait_send()
        for c in range(2):
            out_copy(off, c).wait_send()

    def w_sent(t, carry):
        w_copy(t).wait_send()
        return carry

    lax.fori_loop(0, blocks * (width - 1), w_sent, 0)


HALVES = 2
STEP = 16


def per_device_rows(green_irr, screened, kmap, rotation):
    halves = lax.axis_size("kh")
    width = lax.axis_size("kl")
    total = halves * width
    zone, basis = rotation.shape
    rows = green_irr.shape[2]
    part = rows // width
    sites = part // ORB
    near = screened.shape[0]
    here = near * width
    count = total * ORB
    order = column_order(basis)

    place = jnp.arange(near * STEP, dtype=jnp.int32)
    swap = ((place % near * STEP + place // near)[:, None] == place[None, :]).astype(jnp.bfloat16)
    place = jnp.arange(total * part, dtype=jnp.int32)
    origin = place % part // ORB * count + place // part * ORB + place % ORB
    site = (origin[:, None] == place[None, :]).astype(jnp.bfloat16)

    cos_t, sin_t = phase_tables(zone)
    first_r = lax.axis_index("kh") * here
    forth = jnp.concatenate([cos_t, -sin_t], axis=1)
    forth = lax.dynamic_slice_in_dim(forth, first_r, here, 0)
    back_t = jnp.concatenate([cos_t, -sin_t], axis=0)
    back_t = lax.dynamic_slice_in_dim(back_t, first_r, here, 1)

    source = jnp.where(rotation >= 0, rotation, -1 - rotation)
    place = source - (jnp.arange(basis, dtype=jnp.int32) // ORB * ORB)[None, :] + 1
    code = jnp.where(rotation >= 0, place, -place).astype(jnp.bfloat16)
    code = jnp.dot(code, order, preferred_element_type=jnp.float32).astype(jnp.bfloat16)
    first = lax.axis_index("ba") * rows + lax.axis_index("kl") * part
    row_place = lax.dynamic_slice_in_dim(place, first, part, 1) + kmap * ORB
    row_turn = lax.dynamic_slice_in_dim(rotation, first, part, 1)
    row_code = jnp.where(row_turn >= 0, row_place, -row_place).astype(jnp.float32)
    row_code = row_code.T.reshape(sites, ORB, zone)
    targets = kmap.reshape(1, zone)

    bf16 = jnp.bfloat16
    vmem = pl.BlockSpec(memory_space=pltpu.VMEM)
    copies = part // STEP * (width - 1)
    out = pl.pallas_call(
        functools.partial(kernel, halves, width),
        in_specs=[vmem] * 10,
        out_specs=vmem,
        out_shape=jax.ShapeDtypeStruct((2, rows, basis), jnp.float32),
        scratch_shapes=[
            pltpu.VMEM((width, 2, part, basis), bf16),
            pltpu.VMEM((total, 2, part, basis), bf16),
            pltpu.VMEM((sites, count, 2 * basis), bf16),
            pltpu.VMEM((width, part, near, basis), bf16),
            pltpu.VMEM((width, part, near, basis), bf16),
            pltpu.VMEM((part, here, basis), bf16),
            pltpu.VMEM((ORB, ORB, zone, basis // ORB), bf16),
            pltpu.VMEM((ORB * zone, 2 * basis), bf16),
            pltpu.VMEM((ORB, 2 * zone, basis), bf16),
            pltpu.VMEM((2, sites, count, basis), bf16),
            pltpu.VMEM((total, 2, part, basis), bf16),
            pltpu.VMEM((total, 2, part, basis), bf16),
            pltpu.SemaphoreType.DMA((total - 1,)),
            pltpu.SemaphoreType.DMA((total - 1,)),
            pltpu.SemaphoreType.DMA((copies,)),
            pltpu.SemaphoreType.DMA((copies,)),
            pltpu.SemaphoreType.DMA((2, total - 1)),
            pltpu.SemaphoreType.DMA((2, total - 1)),
        ],
        compiler_params=pltpu.CompilerParams(
            collective_id=0, has_side_effects=True, vmem_limit_bytes=52 << 20
        ),
        cost_estimate=pl.CostEstimate(
            flops=60000000000, bytes_accessed=12 << 20, transcendentals=0
        ),
    )(
        swap, order, site, green_irr.reshape(2 * rows, basis), screened, row_code, targets,
        code, forth, back_t,
    )
    return out.reshape(1, 2, rows, basis)


def solution(mesh):
    sizes = mesh.shape
    width, lines = sizes["ka"], sizes["ba"]
    columns = (P("ka", None, "ba", None), P("ka", "ba", None), P(), P())

    def run(green_irr, screened, kmap, rotation):
        rows = green_irr.shape[2] // lines
        near = screened.shape[0] // width
        parts = width // HALVES
        if green_irr.shape[0] != width or width % HALVES or rows % (parts * ORB * 8) or near % 16:
            return jax.shard_map(
                per_device_columns,
                mesh=mesh,
                in_specs=columns,
                out_specs=P("ka", None, "ba", None),
                check_vma=False,
            )(green_irr, screened, kmap, rotation)
        finer = Mesh(mesh.devices.reshape(HALVES, parts, lines), ("kh", "kl", "ba"))
        both = ("kh", "kl")
        placed = (P(both, None, "ba", None), P(both, "ba", None), P(), P())
        return jax.shard_map(
            per_device_rows,
            mesh=finer,
            in_specs=placed,
            out_specs=P(both, None, "ba", None),
            check_vma=False,
        )(green_irr, screened, kmap, rotation)

    return run
```
